32 devices in a mesh: cluster: 16 (over z, y, x), copy: 2 (over core).
Axes of the slice: x: 2, y: 2, z: 4, core: 2. Of those that a mesh axis runs over, the one named last changes fastest.
Arguments:
- points: bfloat16 [512, 128, 512], P(('cluster', 'copy')), may hold values from -18 to 18
- block_ids: int32 [512], P(('cluster', 'copy')), may hold values from 0 to 15, as said below
- block_counts: int32 [32], P(('cluster', 'copy')), may hold values from 11 to 16, as said below
- centroids: bfloat16 [32768, 512], P('cluster'), may hold values from -6 to 6
Outputs:
- new_centroids: bfloat16 [32768, 512], P(('cluster', 'copy'))
The draws below stay inside these ranges and needn't reach their ends.
Inputs may be any that keep to these rules, and one draw needn't show every extreme that they name: `block_ids`: the 16 blocks of one device name 16 different coarse clusters. For every index along copy, one coarse cluster is named by the first block of every device with that copy index. Only the first block_counts[d] block slots of device d are valid. Some device has all 16 valid.
All inputs are finite; a program needn't handle non-finite values.
Results may differ from the reference program's by a relative error of at most 0.0021.
Values may be sent and summed in bfloat16 or wider, within the bound.
No kernel may reach another device: no remote copies, remote signals or barrier semaphores. Data moves between devices by JAX's collectives and lax.ppermute only.
A program may use at most 64 MiB of HBM per device.

```python
import math
import jax
import jax.numpy as jnp
from jax import lax

D = 512
K = 2048
BLOCK = 128
NB = 16
N_CLUSTER = 16
N_COPY = 2
DEVICES = 32


def route_table(key):
    favorite = jax.random.randint(jax.random.fold_in(key, 101), (N_COPY,), 0, N_CLUSTER)
    levels = jax.random.randint(jax.random.fold_in(key, 102), (N_CLUSTER,), 1, 5)
    lottery = jax.random.randint(jax.random.fold_in(key, 103), (DEVICES, N_CLUSTER), 0, 65536)
    owner_ids = jnp.arange(N_CLUSTER, dtype=jnp.int32)
    scores = lottery * levels[None, :] * N_CLUSTER + owner_ids[None, :]
    replica = jnp.arange(DEVICES, dtype=jnp.int32) % N_COPY
    preferred = owner_ids[None, :] == favorite[replica][:, None]
    scores = jnp.where(preferred, jnp.int32(1 << 30), scores).astype(jnp.int32)
    chosen = lax.top_k(scores, NB)[1].astype(jnp.int32)
    return chosen


def draw_block_ids(key, part):
    return route_table(key).reshape(DEVICES * NB)


def draw_block_counts(key, part):
    lowest = NB - NB * 5 // 16
    counts_drawn = jax.random.randint(jax.random.fold_in(key, 104), (DEVICES,), lowest, NB + 1)
    fullest = jax.random.randint(jax.random.fold_in(key, 105), (), 0, DEVICES)
    return jnp.where(jnp.arange(DEVICES) == fullest, NB, counts_drawn).astype(jnp.int32)


def draw_centroids(key, part):
    normal_draw = jax.random.normal(jax.random.fold_in(key, 108), (N_CLUSTER * K, D), jnp.float32)
    return jnp.clip(normal_draw, -6.0, 6.0).astype(jnp.bfloat16)


def draw_points(key, part):
    extent = (DEVICES * NB, BLOCK, D)
    normal_draw = jax.random.normal(jax.random.fold_in(key, 113), extent, jnp.float32)
    return jnp.clip(normal_draw, -6.0, 6.0).astype(jnp.bfloat16)


def setup_inputs(seed: int = 0) -> dict:
    splits = jax.random.split(jax.random.key(seed), 5)
    points = draw_points(jax.random.fold_in(splits[4], 71), 0)
    block_ids = draw_block_ids(jax.random.fold_in(splits[4], 71), 0)
    block_counts = draw_block_counts(jax.random.fold_in(splits[4], 71), 0)
    centroids = draw_centroids(jax.random.fold_in(splits[4], 71), 0)
    return {"points": points, "block_ids": block_ids, "block_counts": block_counts, "centroids": centroids}


turn_blocks = 4

def cluster_sums(points, block_ids, block_counts, cluster_rows, cluster):
    devices_all = block_counts.shape[0]
    id_table = block_ids.reshape(devices_all, NB)
    slot_index = jnp.arange(NB, dtype=jnp.int32)
    in_range = slot_index[None, :] < block_counts[:, None]
    matches = (id_table == cluster) & in_range
    holder = jnp.any(matches, axis=1)
    position = lax.optimization_barrier(jnp.sum(jnp.where(matches, slot_index[None, :], 0), axis=1)).astype(jnp.int32)
    flat_index = (jnp.arange(devices_all, dtype=jnp.int32) * NB + position).astype(jnp.int32)
    ranking = (jnp.cumsum(holder.astype(jnp.int32)) - 1).astype(jnp.int32)
    listing = jnp.zeros((devices_all + turn_blocks,), jnp.int32)
    listing = listing.at[jnp.where(holder, ranking, devices_all + turn_blocks)].set(flat_index, mode='drop')
    how_many = jnp.sum(holder.astype(jnp.int32)).astype(jnp.int32)
    scale_factor = 3.0 / math.sqrt(D)

    def visit(step_index, running):
        start_at = (step_index * turn_blocks).astype(jnp.int32)
        chosen = lax.dynamic_slice_in_dim(listing, start_at, turn_blocks)
        usable = start_at + jnp.arange(turn_blocks, dtype=jnp.int32) < how_many
        gathered = points[chosen].reshape(turn_blocks * BLOCK, D)
        logits = jnp.dot(gathered, cluster_rows.T, preferred_element_type=jnp.float32) * scale_factor
        row_mask = jnp.repeat(usable, BLOCK).astype(jnp.float32)[:, None]
        weights = (jax.nn.softmax(logits, axis=-1) * row_mask).astype(jnp.bfloat16)
        return running + jnp.dot(weights.T, gathered, preferred_element_type=jnp.float32)
    initial = jnp.zeros((K, D), jnp.float32)
    upper = ((how_many + turn_blocks - 1) // turn_blocks).astype(jnp.int32)
    return lax.fori_loop(jnp.int32(0), upper, visit, initial)

def reference(points, block_ids, block_counts, centroids):
    grouped = centroids.reshape(N_CLUSTER, K, D)

    def per_cluster(cluster):
        cluster_rows = grouped[cluster]
        summed = cluster_sums(points, block_ids, block_counts, cluster_rows, cluster)
        combined = summed + cluster_rows.astype(jnp.float32)
        scaled = combined * lax.rsqrt(lax.optimization_barrier(jnp.mean(combined * combined, axis=-1, keepdims=True)) + 1e-06)
        return scaled.astype(jnp.bfloat16)
    updated = lax.map(per_cluster, jnp.arange(N_CLUSTER, dtype=jnp.int32))
    return updated.reshape(N_CLUSTER * K, D)
```

```python
import functools
import math

import jax
import jax.numpy as jnp
from jax import lax
from jax.experimental import pallas as pl
from jax.experimental.pallas import tpu as pltpu
from jax.sharding import PartitionSpec as P

F32 = jnp.float32
BF16 = jnp.bfloat16
TILE = 256
TURN = 4
MIB = 1 << 20


def partner(index, offset, size):
    if size & (size - 1) == 0:
        return index ^ offset
    return lax.rem(index + offset, size) if not isinstance(index, int) else (index + offset) % size


def pairs(offset, size):
    return [(i, partner(i, offset, size)) for i in range(size)]


def stage_kernel(owners, ids, counts, points, *refs):
    outs, (where, zeros, sems) = refs[:owners], refs[owners:]
    slots = points.shape[0]
    me = lax.axis_index("cluster")
    zeros[...] = jnp.zeros_like(zeros)
    for o in range(owners):
        where[o] = -1
    for s in range(slots):

        @pl.when(s < counts[0])
        def _():
            where[ids[s]] = s

    for k in range(owners):
        slot = where[partner(me, k, owners)]

        @pl.when(slot >= 0)
        def _():
            pltpu.make_async_copy(points.at[jnp.maximum(slot, 0)], outs[k], sems.at[k]).start()

        @pl.when(slot < 0)
        def _():
            pltpu.make_async_copy(zeros, outs[k], sems.at[k]).start()

    for k in range(owners):
        pltpu.make_async_copy(zeros, outs[k], sems.at[k]).wait()


def stage(points, ids, counts, owners):
    block = points.shape[1:]
    return pl.pallas_call(
        functools.partial(stage_kernel, owners),
        out_shape=[jax.ShapeDtypeStruct(block, points.dtype)] * owners,
        in_specs=[
            pl.BlockSpec(memory_space=pltpu.SMEM),
            pl.BlockSpec(memory_space=pltpu.SMEM),
            pl.BlockSpec(memory_space=pl.ANY),
        ],
        out_specs=[pl.BlockSpec(memory_space=pl.ANY)] * owners,
        scratch_shapes=[
            pltpu.SMEM((owners,), jnp.int32),
            pltpu.VMEM(block, points.dtype),
            pltpu.SemaphoreType.DMA((owners,)),
        ],
        name="stage",
    )(ids, counts, points)


def sums_kernel(blocks, replicas, parts, earlier, last, *refs):
    xs, rest = refs[:blocks], refs[blocks:]
    cents, rest = rest[0], rest[1:]
    befores, rest = rest[: parts * earlier], rest[parts * earlier :]
    outs, rest = rest[:parts], rest[parts:]
    cv, xv, lt, av, bv, ov, sx, sc, sb, so = rest
    total, feature = cv.shape
    rows = xs[0].shape[0]
    share = total // replicas
    tile = min(TILE, share)
    tiles = share // tile
    scale = 3.0 / math.sqrt(feature) * math.log2(math.e)
    me = lax.axis_index("copy")

    x_copies = [
        pltpu.make_async_copy(xs[b], xv.at[pl.ds(b * rows, rows)], sx.at[b]) for b in range(blocks)
    ]
    for copy in x_copies:
        copy.start()
    c_copies = []
    for q in range(replicas):
        start = lax.rem(me + q, replicas) * share
        for t in range(tiles):
            i = q * tiles + t
            c_copies.append(
                pltpu.make_async_copy(
                    cents.at[pl.ds(pl.multiple_of(start + t * tile, tile), tile)],
                    cv.at[pl.ds(i * tile, tile)],
                    sc.at[i],
                )
            )
    for copy in c_copies:
        copy.start()
    b_copies = []
    for e in range(earlier):
        for q in range(parts):
            i = e * parts + q
            b_copies.append(
                pltpu.make_async_copy(befores[i], bv.at[pl.ds(i * share, share)], sb.at[i])
            )
    for copy in b_copies:
        copy.start()

    out_copies = []
    for first in range(0, blocks, TURN):
        some = min(TURN, blocks - first)
        n = some * rows
        for copy in x_copies[first : first + some]:
            copy.wait()
        x = xv[pl.ds(first * rows, n), :]
        xt = x.T
        high = jnp.full((8, n), -jnp.inf, F32)
        for i in range(total // tile):
            if first == 0:
                c_copies[i].wait()
            logits = jnp.dot(cv[pl.ds(i * tile, tile), :], xt, preferred_element_type=F32)
            lt[pl.ds(i * tile, tile), pl.ds(0, n)] = logits
            high = jnp.maximum(high, jnp.max(logits.reshape(tile // 8, 8, n), axis=0))
        high = jnp.max(high, axis=0, keepdims=True) * scale
        norm = jnp.zeros((8, n), F32)
        for i in range(total // tile):
            e = jnp.exp2(lt[pl.ds(i * tile, tile), pl.ds(0, n)] * scale - high)
            lt[pl.ds(i * tile, tile), pl.ds(0, n)] = e
            norm = norm + jnp.sum(e.reshape(tile // 8, 8, n), axis=0)
        inverse = 1.0 / jnp.sum(norm, axis=0, keepdims=True)
        for q in reversed(range(parts)):
            if first == 0:
                for e in range(earlier):
                    b_copies[e * parts + q].wait()
            for t in range(tiles):
                i = q * tiles + t
                here = pl.ds(i * tile, tile)
                weights = (lt[here, pl.ds(0, n)] * inverse).astype(BF16)
                s = jnp.dot(weights, x, preferred_element_type=F32)
                if first == 0:
                    for e in range(earlier):
                        s = s + bv[pl.ds((e * parts + q) * share + t * tile, tile), :]
                else:
                    s = s + av[here, :]
                if first + some < blocks:
                    av[here, :] = s
                    continue
                if last:
                    v = s + cv[here, :].astype(F32)
                    mean = jnp.mean(v * v, axis=-1, keepdims=True)
                    ov[here, :] = (v * lax.rsqrt(mean + 1e-06)).astype(BF16)
                    source = ov
                else:
                    av[here, :] = s
                    source = av
                copy = pltpu.make_async_copy(
                    source.at[here], outs[q].at[pl.ds(t * tile, tile)], so.at[i]
                )
                copy.start()
                out_copies.append(copy)
    for copy in out_copies:
        copy.wait()


def sums(xs, centroids, befores, replicas, parts, last=False):
    blocks = len(xs)
    rows, feature = xs[0].shape
    total = centroids.shape[0]
    share = total // replicas
    tile = min(TILE, share)
    earlier = len(befores) // parts
    points = blocks * rows
    any_spec = pl.BlockSpec(memory_space=pl.ANY)
    out = jax.ShapeDtypeStruct((share, feature), BF16 if last else F32)
    small = (8, feature)
    return pl.pallas_call(
        functools.partial(sums_kernel, blocks, replicas, parts, earlier, last),
        out_shape=[out] * parts,
        in_specs=[any_spec] * (blocks + 1 + len(befores)),
        out_specs=[any_spec] * parts,
        scratch_shapes=[
            pltpu.VMEM((total, feature), BF16),
            pltpu.VMEM((points, feature), BF16),
            pltpu.VMEM((total, min(TURN, blocks) * rows), F32),
            pltpu.VMEM((parts * share, feature), F32),
            pltpu.VMEM((max(len(befores), 1) * share, feature), F32),
            pltpu.VMEM((parts * share, feature) if last else (16, feature), BF16),
            pltpu.SemaphoreType.DMA((blocks,)),
            pltpu.SemaphoreType.DMA((total // tile,)),
            pltpu.SemaphoreType.DMA((max(len(befores), 1),)),
            pltpu.SemaphoreType.DMA((parts * share // tile,)),
        ],
        compiler_params=pltpu.CompilerParams(vmem_limit_bytes=48 * MIB),
        cost_estimate=pl.CostEstimate(
            flops=2 * points * feature * (total + parts * share),
            bytes_accessed=2 * total * feature + 2 * points * feature + 4 * parts * share * feature,
            transcendentals=points * total,
        ),
        name="last_sums" if last else "sums",
    )(*xs, centroids, *befores)


def local(points, block_ids, block_counts, centroids):
    owners = lax.axis_size("cluster")
    replicas = lax.axis_size("copy")
    staged = stage(points, block_ids, block_counts, owners)

    half = owners // 2
    near, far = list(range(1, half)), list(range(half, owners))
    order = []
    for i in range(max(len(near), len(far))):
        order += far[i : i + 1] + near[i : i + 1]
    arrived = {0: staged[0]}
    for k in order:
        arrived[k] = lax.ppermute(staged[k], "cluster", pairs(k, owners))

    def others(array, r):
        return lax.ppermute(array, "copy", [(i, (i + r) % replicas) for i in range(replicas)])

    def everyone(blocks):
        return blocks + [others(b, r) for r in range(1, replicas) for b in blocks]

    cut = max(len(far) - 3, 1)
    first = [arrived[0]] + [arrived[k] for k in near]
    second = [arrived[k] for k in far[:cut]]
    third = [arrived[k] for k in far[cut:-1]]
    fourth = [arrived[far[-1]]]

    early = sums(first, centroids, [], replicas, replicas)
    early = sums(second, centroids, early, replicas, replicas)
    mine = [early[0]] + [others(early[r], r) for r in range(1, replicas)]
    mine = sums(everyone(third), centroids, mine, replicas, 1)
    return sums(everyone(fourth), centroids, mine, replicas, 1, last=True)[0]


def solution(mesh):
    return jax.shard_map(
        local,
        mesh=mesh,
        in_specs=(
            P(("cluster", "copy"), None, None),
            P(("cluster", "copy")),
            P(("cluster", "copy")),
            P("cluster", None),
        ),
        out_specs=P(("cluster", "copy"), None),
        check_vma=False,
    )
```

```python
import functools
import math

import jax
import jax.numpy as jnp
from jax import lax
from jax.experimental import pallas as pl
from jax.experimental.pallas import tpu as pltpu
from jax.sharding import PartitionSpec as P

F32 = jnp.float32
BF16 = jnp.bfloat16
TILE = 256
TURN = 4
MIB = 1 << 20


def in_hbm(array):
    return pltpu.with_memory_space_constraint(array, pltpu.HBM)


def in_vmem(array):
    return pltpu.with_memory_space_constraint(array, pltpu.VMEM)


def after(array, *others):
    return lax.optimization_barrier((array, *others))[0]


def stage_kernel(offsets, ids_in, counts, points, *refs):
    owners = len(offsets)
    outs, (where, ids, held, zeros, reads, writes, small) = refs[:owners], refs[owners:]
    slots = points.shape[0]
    me = lax.axis_index("cluster")
    ids_copy = pltpu.make_async_copy(ids_in, ids, small)
    ids_copy.start()
    for o in range(owners):
        where[o] = -1
    zeros[...] = jnp.zeros_like(zeros)
    ids_copy.wait()
    for s in range(slots):

        @pl.when(s < counts[0])
        def _():
            where[ids[s]] = s

    for i, k in enumerate(offsets):
        slot = where[me ^ k]

        @pl.when(slot >= 0)
        def _():
            pltpu.make_async_copy(points.at[jnp.maximum(slot, 0)], held.at[i], reads.at[i]).start()

        @pl.when(slot < 0)
        def _():
            pltpu.make_async_copy(zeros, outs[i], writes.at[i]).start()

    for i, k in enumerate(offsets):

        @pl.when(where[me ^ k] >= 0)
        def _():
            pltpu.make_async_copy(points.at[0], held.at[i], reads.at[i]).wait()
            pltpu.make_async_copy(held.at[i], outs[i], writes.at[i]).start()

    for i in range(owners):
        pltpu.make_async_copy(zeros, outs[i], writes.at[i]).wait()


def stage(points, ids, counts, offsets):
    block = points.shape[1:]
    owners = len(offsets)
    spec = pl.BlockSpec(memory_space=pltpu.HBM)
    outs = pl.pallas_call(
        functools.partial(stage_kernel, offsets),
        out_shape=[pltpu.HBM(block, points.dtype)] * owners,
        in_specs=[spec, pl.BlockSpec(memory_space=pltpu.SMEM), spec],
        out_specs=[spec] * owners,
        scratch_shapes=[
            pltpu.SMEM((owners,), jnp.int32),
            pltpu.SMEM(ids.shape, jnp.int32),
            pltpu.VMEM((owners, *block), points.dtype),
            pltpu.VMEM(block, points.dtype),
            pltpu.SemaphoreType.DMA((owners,)),
            pltpu.SemaphoreType.DMA((owners,)),
            pltpu.SemaphoreType.DMA,
        ],
        compiler_params=pltpu.CompilerParams(vmem_limit_bytes=16 * MIB),
        name="stage",
    )(in_hbm(ids), counts, in_hbm(points))
    return dict(zip(offsets, outs))


def sums_kernel(blocks, replicas, send, *refs):
    xs, rest = refs[:blocks], refs[blocks:]
    cents, rest = rest[0], rest[1:]
    befores, outs, lt = rest[: -replicas - 1], rest[-replicas - 1 : -1], rest[-1]
    total, feature = cents.shape
    rows = xs[0].shape[0]
    share = total // replicas
    tile = min(TILE, share)
    scale = 3.0 / math.sqrt(feature) * math.log2(math.e)
    me = lax.axis_index("copy")

    for first in range(0, blocks, TURN):
        some = min(TURN, blocks - first)
        n = some * rows
        x = jnp.concatenate([r[...] for r in xs[first : first + some]], axis=0)
        xt = x.T
        high = jnp.full((8, n), -jnp.inf, F32)
        for i in range(total // tile):
            here = pl.ds(i * tile, tile)
            logits = jnp.dot(cents[here, :], xt, preferred_element_type=F32)
            lt[here, pl.ds(0, n)] = logits
            high = jnp.maximum(high, jnp.max(logits.reshape(tile // 8, 8, n), axis=0))
        high = jnp.max(high, axis=0, keepdims=True) * scale
        norm = jnp.zeros((8, n), F32)
        for i in range(total // tile):
            here = pl.ds(i * tile, tile)
            e = jnp.exp2(lt[here, pl.ds(0, n)] * scale - high)
            lt[here, pl.ds(0, n)] = e
            norm = norm + jnp.sum(e.reshape(tile // 8, 8, n), axis=0)
        inverse = 1.0 / jnp.sum(norm, axis=0, keepdims=True)
        for q in range(replicas):
            start = lax.rem(me + q, replicas) * share
            for t in range(share // tile):
                here = pl.ds(pl.multiple_of(start + t * tile, tile), tile)
                there = pl.ds(t * tile, tile)
                weights = (lt[here, pl.ds(0, n)] * inverse).astype(BF16)
                s = jnp.dot(weights, x, preferred_element_type=F32)
                if first:
                    s = s + outs[q][there, :]
                elif befores:
                    s = s + befores[q][there, :]
                outs[q][there, :] = s.astype(outs[q].dtype)


def sums(xs, centroids, befores, replicas, send=False):
    blocks = len(xs)
    assert blocks <= TURN or not send
    rows, feature = xs[0].shape
    total = centroids.shape[0]
    share = total // replicas
    points = blocks * rows
    spec = pl.BlockSpec(memory_space=pltpu.VMEM)
    outs = [
        jax.ShapeDtypeStruct((share, feature), BF16 if send and q else F32) for q in range(replicas)
    ]
    return pl.pallas_call(
        functools.partial(sums_kernel, blocks, replicas, send),
        out_shape=outs,
        in_specs=[spec] * (blocks + 1 + len(befores)),
        out_specs=[spec] * replicas,
        scratch_shapes=[pltpu.VMEM((total, min(TURN, blocks) * rows), F32)],
        compiler_params=pltpu.CompilerParams(vmem_limit_bytes=28 * MIB),
        cost_estimate=pl.CostEstimate(flops=1024, bytes_accessed=1024, transcendentals=0),
        name="sums",
    )(*xs, centroids, *befores)


def close_kernel(cents, *refs):
    terms, out = refs[:-1], refs[-1]
    share, feature = out.shape
    start = lax.axis_index("copy") * share
    tile = min(TILE, share)
    for t in range(share // tile):
        there = pl.ds(t * tile, tile)
        v = cents[pl.ds(pl.multiple_of(start + t * tile, tile), tile), :].astype(F32)
        for term in terms:
            v = v + term[there, :].astype(F32)
        mean = jnp.mean(v * v, axis=-1, keepdims=True)
        out[there, :] = (v * lax.rsqrt(mean + 1e-06)).astype(BF16)


def close(centroids, terms):
    spec = pl.BlockSpec(memory_space=pltpu.VMEM)
    share, feature = terms[0].shape
    return pl.pallas_call(
        close_kernel,
        out_shape=jax.ShapeDtypeStruct((share, feature), BF16),
        in_specs=[spec] * (1 + len(terms)),
        out_specs=spec,
        compiler_params=pltpu.CompilerParams(vmem_limit_bytes=28 * MIB),
        cost_estimate=pl.CostEstimate(
            flops=8 * share * feature, bytes_accessed=12 * share * feature, transcendentals=share
        ),
        name="close",
    )(centroids, *terms)


def plan(owners):
    half = owners // 2
    near, far = list(range(1, half)), list(range(half, owners))
    groups = [[0] + near[:2]]
    rest = near[2:]
    for i in range(0, len(far) - 2, 2):
        groups.append(far[i : i + 1] + rest[:1] + far[i + 1 : i + 2] + rest[1:2])
        rest = rest[2:]
    return near, far, groups + [[k] for k in far[-2:]]


def local(points, block_ids, block_counts, centroids):
    owners = lax.axis_size("cluster")
    replicas = lax.axis_size("copy")
    assert owners >= 16 and owners & (owners - 1) == 0
    near, far, groups = plan(owners)
    first = [k for pair in zip(far, near) for k in pair]
    rest = [k for k in range(owners) if k not in first]
    staged = stage(points, block_ids, block_counts, first + rest)
    arrived = {0: staged[0]}

    def send(k, *others):
        block = after(staged[k], *others) if others else staged[k]
        arrived[k] = lax.ppermute(block, "cluster", [(d, d ^ k) for d in range(owners)])

    for i, k in enumerate(near):
        send(k, *[arrived[j] for j in near[max(i - 2, 0) : max(i - 1, 0)]])
    for k in far[:3]:
        send(k)
    total, sent = [], 3
    for g, group in enumerate(groups):
        while sent < min(2 * g + 4, len(far)) and g:
            others = [arrived[far[sent - 3]]]
            if sent == 4:
                others.append(arrived[near[3]])
            if sent % 2 == 0 and sent > 4 or sent == 3:
                others.append(total[0])
            send(far[sent], *others)
            sent += 1
        blocks = [arrived[k] for k in group]
        total = sums(blocks, centroids, total, replicas, g == len(groups) - 1)
    received = [
        lax.ppermute(total[r], "copy", [(i, (i + r) % replicas) for i in range(replicas)])
        for r in range(1, replicas)
    ]
    return close(centroids, [total[0]] + received)


def solution(mesh):
    return jax.shard_map(
        local,
        mesh=mesh,
        in_specs=(
            P(("cluster", "copy"), None, None),
            P(("cluster", "copy")),
            P(("cluster", "copy")),
            P("cluster", None),
        ),
        out_specs=P(("cluster", "copy"), None),
        check_vma=False,
    )
```

```python
import functools
import math

import jax
import jax.numpy as jnp
from jax import lax
from jax.experimental import pallas as pl
from jax.experimental.pallas import tpu as pltpu
from jax.sharding import PartitionSpec as P

F32 = jnp.float32
BF16 = jnp.bfloat16
TILE = 512
TURN = 256
MIB = 1 << 20
HALVES = 2


def in_hbm(array):
    return pltpu.with_memory_space_constraint(array, pltpu.HBM)


def in_vmem(array):
    return pltpu.with_memory_space_constraint(array, pltpu.VMEM)


def after(array, *others):
    return lax.optimization_barrier((array, *others))[0]


def stage_kernel(alone, paired, ids_in, counts, points, *refs):
    singles, rest = refs[: len(alone)], refs[len(alone) :]
    keeps, (give, where, ids, held, zeros, reads, writes, small) = rest[: len(paired)], rest[len(paired) :]
    slots, rows = points.shape[:2]
    me, core = lax.axis_index("cluster"), lax.rem(lax.axis_index("copy"), 2)
    ids_copy = pltpu.make_async_copy(ids_in, ids, small)
    ids_copy.start()
    for s in range(slots):
        pltpu.make_async_copy(points.at[s], held.at[s], reads.at[s]).start()
    for o in range(where.shape[0]):
        where[o] = -1
    zeros[...] = jnp.zeros_like(zeros)
    ids_copy.wait()
    for s in range(slots):

        @pl.when(s < counts[0])
        def _():
            where[ids[s]] = s

    for s in range(slots):
        pltpu.make_async_copy(points.at[s], held.at[s], reads.at[s]).wait()
    targets = [(k, out) for k, out in zip(alone, singles)]
    targets += [(k + 1 - core, give.at[pl.ds(i * rows, rows)]) for i, k in enumerate(paired)]
    targets += [(k + core, out.at[pl.ds(0, rows)]) for k, out in zip(paired, keeps)]
    for i, (k, out) in enumerate(targets):
        slot = where[me ^ k]

        @pl.when(slot >= 0)
        def _():
            pltpu.make_async_copy(held.at[jnp.maximum(slot, 0)], out, writes.at[i]).start()

        @pl.when(slot < 0)
        def _():
            pltpu.make_async_copy(zeros, out, writes.at[i]).start()

    for i, (k, out) in enumerate(targets):
        pltpu.make_async_copy(zeros, out, writes.at[i]).wait()


def stage(points, ids, counts, owners, alone, paired):
    rows, feature = points.shape[1:]
    spec = pl.BlockSpec(memory_space=pltpu.HBM)
    hbm = lambda n: pltpu.HBM((n, feature), points.dtype)
    outs = pl.pallas_call(
        functools.partial(stage_kernel, alone, paired),
        out_shape=[hbm(rows)] * len(alone) + [hbm(2 * rows)] * len(paired) + [hbm(len(paired) * rows)],
        in_specs=[spec, pl.BlockSpec(memory_space=pltpu.SMEM), spec],
        out_specs=[spec] * (len(alone) + len(paired) + 1),
        scratch_shapes=[
            pltpu.SMEM((owners,), jnp.int32),
            pltpu.SMEM(ids.shape, jnp.int32),
            pltpu.VMEM(points.shape, points.dtype),
            pltpu.VMEM((rows, feature), points.dtype),
            pltpu.SemaphoreType.DMA((points.shape[0],)),
            pltpu.SemaphoreType.DMA((len(alone) + 2 * len(paired),)),
            pltpu.SemaphoreType.DMA,
        ],
        compiler_params=pltpu.CompilerParams(vmem_limit_bytes=16 * MIB),
        name="stage",
    )(in_hbm(ids), counts, in_hbm(points))
    return dict(zip(alone, outs)), dict(zip(paired, outs[len(alone) : -1])), outs[-1]


def merge_kernel(got, *refs):
    outs, sems = refs[len(refs) // 2 : -1], refs[-1]
    rows = got.shape[0] // len(outs)
    copies = [
        pltpu.make_async_copy(got.at[pl.ds(i * rows, rows)], out.at[pl.ds(rows, rows)], sems.at[i])
        for i, out in enumerate(outs)
    ]
    for copy in copies:
        copy.start()
    for copy in copies:
        copy.wait()


def merge(keeps, got):
    spec = pl.BlockSpec(memory_space=pltpu.HBM)
    return pl.pallas_call(
        merge_kernel,
        out_shape=[pltpu.HBM(k.shape, k.dtype) for k in keeps],
        in_specs=[pl.BlockSpec(memory_space=pltpu.VMEM)] + [spec] * len(keeps),
        out_specs=[spec] * len(keeps),
        input_output_aliases={1 + i: i for i in range(len(keeps))},
        scratch_shapes=[pltpu.SemaphoreType.DMA((len(keeps),))],
        compiler_params=pltpu.CompilerParams(vmem_limit_bytes=16 * MIB),
        name="merge",
    )(in_vmem(got), *keeps)


def turns(xs):
    found, left = [], 0
    for i, x in enumerate(xs):
        start = 0
        while start < x.shape[0]:
            if not left:
                found.append([])
                left = TURN
            size = min(left, x.shape[0] - start)
            found[-1].append((i, start, start + size))
            start, left = start + size, left - size
    return found


def sums_kernel(blocks, replicas, last, *refs):
    xs, rest = refs[:blocks], refs[blocks:]
    cents, rest = rest[0], rest[1:]
    results = (1 + (replicas - 1) * HALVES) if last else replicas
    befores, outs, lts = rest[: -results - 2], rest[-results - 2 : -2], rest[-2:]
    total, feature = cents.shape
    share = total // replicas
    tile = min(TILE, share // HALVES if last else share)
    tiles = total // tile
    scale = 3.0 / math.sqrt(feature) * math.log2(math.e)
    me = lax.axis_index("copy")

    def logits(i, x, lt, high):
        here = pl.ds(i * tile, tile)
        n = x.shape[0]
        l = jnp.dot(cents[here, :], x.T, preferred_element_type=F32)
        lt[here, pl.ds(0, n)] = l
        return jnp.maximum(high, jnp.max(l.reshape(tile // 8, 8, n), axis=0))

    def exponentials(i, lt, high, norm):
        here, n = pl.ds(i * tile, tile), high.shape[1]
        e = jnp.exp2(lt[here, pl.ds(0, n)] * scale - high)
        lt[here, pl.ds(0, n)] = e
        return norm + jnp.sum(e.reshape(tile // 8, 8, n), axis=0)

    def add(i, x, lt, inverse, fresh):
        q, t = i // (share // tile), i % (share // tile)
        here = pl.ds(pl.multiple_of(lax.rem(me + q, replicas) * share + t * tile, tile), tile)
        there = pl.ds(t * tile, tile)
        weights = (lt[here, pl.ds(0, x.shape[0])] * inverse).astype(BF16)
        if last and not q:
            outs[0][there, :] = weights
            return
        s = jnp.dot(weights, x, preferred_element_type=F32)
        if not fresh:
            s = s + outs[q][there, :]
        elif befores:
            s = s + befores[q][there, :]
        if last:
            size = share // HALVES
            outs[1 + (q - 1) * HALVES + t * tile // size][pl.ds(t * tile % size, tile), :] = s
        else:
            outs[q][there, :] = s

    waiting = None
    for first, pieces in enumerate(turns(xs)):
        x = jnp.concatenate([xs[i][a:b, :] for i, a, b in pieces], axis=0)
        lt = lts[first % 2]
        n = x.shape[0]
        high = jnp.full((8, n), -jnp.inf, F32)
        if waiting:
            px, plt, phigh, fresh = waiting
            pnorm = jnp.zeros((8, px.shape[0]), F32)
        for i in range(tiles):
            high = logits(i, x, lt, high)
            if waiting:
                pnorm = exponentials(i, plt, phigh, pnorm)
        if waiting:
            inverse = 1.0 / jnp.sum(pnorm, axis=0, keepdims=True)
            for i in range(tiles):
                add(i, px, plt, inverse, fresh)
        high = jnp.max(high, axis=0, keepdims=True) * scale
        waiting = x, lt, high, first == 0
    x, lt, high, fresh = waiting
    norm = jnp.zeros((8, x.shape[0]), F32)
    for i in range(tiles):
        norm = exponentials(i, lt, high, norm)
    inverse = 1.0 / jnp.sum(norm, axis=0, keepdims=True)
    for i in range(tiles):
        add(i, x, lt, inverse, fresh)


def sums(xs, centroids, befores, replicas, last=False):
    total, feature = centroids.shape
    share = total // replicas
    points = sum(x.shape[0] for x in xs)
    assert points <= TURN or not last
    spec = pl.BlockSpec(memory_space=pltpu.VMEM)
    outs = [jax.ShapeDtypeStruct((share, feature), F32)] * replicas
    if last:
        outs = [jax.ShapeDtypeStruct((share, points), BF16)]
        outs += [jax.ShapeDtypeStruct((share // HALVES, feature), F32)] * ((replicas - 1) * HALVES)
    return pl.pallas_call(
        functools.partial(sums_kernel, len(xs), replicas, last),
        out_shape=outs,
        in_specs=[spec] * (len(xs) + 1 + len(befores)),
        out_specs=[spec] * len(outs),
        scratch_shapes=[pltpu.VMEM((total, min(TURN, points)), F32)] * 2,
        compiler_params=pltpu.CompilerParams(vmem_limit_bytes=28 * MIB),
        cost_estimate=pl.CostEstimate(flops=1024, bytes_accessed=1024, transcendentals=0),
        name="sums",
    )(*xs, centroids, *befores)


def own_kernel(blocks, *refs):
    xs, (weights, before, cents, out) = refs[:blocks], refs[blocks:]
    share = out.shape[0]
    tile = min(TILE, share)
    x = jnp.concatenate([r[...] for r in xs], axis=0)
    for t in range(share // tile):
        there = pl.ds(t * tile, tile)
        here = pl.ds(pl.multiple_of(lax.axis_index("copy") * share + t * tile, tile), tile)
        s = jnp.dot(weights[there, :], x, preferred_element_type=F32)
        out[there, :] = s + before[there, :] + cents[here, :].astype(F32)


def own(xs, weights, before, centroids):
    spec = pl.BlockSpec(memory_space=pltpu.VMEM)
    return pl.pallas_call(
        functools.partial(own_kernel, len(xs)),
        out_shape=jax.ShapeDtypeStruct(before.shape, F32),
        in_specs=[spec] * (len(xs) + 3),
        out_specs=spec,
        compiler_params=pltpu.CompilerParams(vmem_limit_bytes=28 * MIB),
        cost_estimate=pl.CostEstimate(flops=1024, bytes_accessed=1024, transcendentals=0),
        name="own",
    )(*xs, weights, before, centroids)


def close_kernel(h, terms, own, *refs):
    received, (out, held, sems) = refs[:terms], refs[-3:]
    size, feature = received[0].shape
    tile = size // 2
    copies = []
    for t in range(size // tile):
        there = pl.ds(t * tile, tile)
        v = own[pl.ds(h * size + t * tile, tile), :]
        for term in received:
            v = v + term[there, :]
        mean = jnp.mean(v * v, axis=-1, keepdims=True)
        held[there, :] = (v * lax.rsqrt(mean + 1e-06)).astype(BF16)
        copies.append(pltpu.make_async_copy(held.at[there], out.at[pl.ds(h * size + t * tile, tile)], sems.at[t]))
        copies[-1].start()
    for copy in copies:
        copy.wait()


def close(own, received, out, h):
    vmem, hbm = pl.BlockSpec(memory_space=pltpu.VMEM), pl.BlockSpec(memory_space=pl.ANY)
    terms = len(received)
    return pl.pallas_call(
        functools.partial(close_kernel, h, terms),
        out_shape=jax.ShapeDtypeStruct(own.shape, BF16),
        in_specs=[vmem] * (1 + terms) + [hbm] * len(out),
        out_specs=hbm,
        input_output_aliases={1 + terms: 0} if out else {},
        scratch_shapes=[pltpu.VMEM(received[0].shape, BF16), pltpu.SemaphoreType.DMA((2,))],
        compiler_params=pltpu.CompilerParams(vmem_limit_bytes=28 * MIB),
        cost_estimate=pl.CostEstimate(flops=1024, bytes_accessed=1024, transcendentals=0),
        name="close",
    )(own, *received, *out)


def local(points, block_ids, block_counts, centroids):
    owners = lax.axis_size("cluster")
    replicas = lax.axis_size("copy")
    assert owners >= 16 and owners & (owners - 1) == 0 and replicas % 2 == 0
    half = owners // 2
    far, paired = list(range(half, owners)), list(range(2, half, 2))
    singles, keeps, give = stage(points, block_ids, block_counts, owners, far + [0, 1], paired)
    give = lax.ppermute(give, "copy", [(k, k ^ 1) for k in range(replicas)])
    both = merge([keeps[k] for k in paired], give)
    arrived = {0: singles[0]}

    def send(k, *others):
        array = singles[k] if k in singles else both[paired.index(k)]
        pairs = []
        for d in range(owners):
            for r in range(replicas):
                to = d ^ (k + r % 2 if k in paired else k)
                pairs.append((d * replicas + r, to * replicas + r))
        array = after(array, *others) if others else array
        arrived[k] = lax.ppermute(array, ("cluster", "copy"), pairs)

    groups = [[0, 1, paired[0]]]
    for i in range(0, len(far) - 2, 2):
        groups.append(far[i : i + 2] + paired[1 + i // 2 : 2 + i // 2])
    groups += [far[-2:-1], far[-1:]]
    totals = []

    def work():
        group = groups[len(totals)]
        for k in group:
            if k not in arrived:
                i = paired.index(k) if k in paired else 0
                send(k, *([arrived[1 if i < 3 else paired[i - 3]]] if i else []))
        before = totals[-1] if totals else []
        last = len(totals) == len(groups) - 1
        totals.append(sums([arrived[k] for k in group], centroids, before, replicas, last))

    for i, k in enumerate(far):
        others = [arrived[far[i - 3]]] if i >= 3 else []
        if i >= 6:
            ahead = min(i - 6, i // 2 - 2)
            while len(totals) <= ahead:
                work()
            others.append(totals[ahead][0])
        send(k, *others)
    while len(totals) < len(groups):
        work()
    before, (weights, *shares) = totals[-2:]

    mine = own([arrived[k] for k in groups[-1]], weights, before[0], centroids)
    received = []
    for h in range(HALVES):
        received.append([
            lax.ppermute(shares[(r - 1) * HALVES + h], "copy", [(i, (i + r) % replicas) for i in range(replicas)])
            for r in range(1, replicas)
        ])
    out = []
    for h in range(HALVES):
        out = [close(mine, received[h], out, h)]
    return out[0]


def solution(mesh):
    return jax.shard_map(
        local,
        mesh=mesh,
        in_specs=(
            P(("cluster", "copy"), None, None),
            P(("cluster", "copy")),
            P(("cluster", "copy")),
            P("cluster", None),
        ),
        out_specs=P(("cluster", "copy"), None),
        check_vma=False,
    )
```

```python
import functools
import math

import jax
import jax.numpy as jnp
from jax import lax
from jax.experimental import pallas as pl
from jax.experimental.pallas import tpu as pltpu
from jax.sharding import PartitionSpec as P

F32 = jnp.float32
BF16 = jnp.bfloat16
TILE = 512
TURN = 256
MIB = 1 << 20
HALVES = 2


def in_hbm(array):
    return pltpu.with_memory_space_constraint(array, pltpu.HBM)


def in_vmem(array):
    return pltpu.with_memory_space_constraint(array, pltpu.VMEM)


def after(array, *others):
    return lax.optimization_barrier((array, *others))[0]


def stage_kernel(alone, paired, ids_in, counts, points, *refs):
    singles, rest = refs[: len(alone)], refs[len(alone) :]
    keeps, (give, where, ids, held, zeros, reads, writes, small) = rest[: len(paired)], rest[len(paired) :]
    slots, rows = points.shape[:2]
    me, core = lax.axis_index("cluster"), lax.rem(lax.axis_index("copy"), 2)
    ids_copy = pltpu.make_async_copy(ids_in, ids, small)
    ids_copy.start()
    for s in range(slots):
        pltpu.make_async_copy(points.at[s], held.at[s], reads.at[s]).start()
    for o in range(where.shape[0]):
        where[o] = -1
    zeros[...] = jnp.zeros_like(zeros)
    ids_copy.wait()
    for s in range(slots):

        @pl.when(s < counts[0])
        def _():
            where[ids[s]] = s

    targets = [(k, out) for k, out in zip(alone, singles)]
    targets += [(k + 1 - core, give.at[pl.ds(i * rows, rows)]) for i, k in enumerate(paired)]
    targets += [(k + core, out.at[pl.ds(0, rows)]) for k, out in zip(paired, keeps)]
    for i, (k, out) in enumerate(targets):
        slot = where[me ^ k]

        @pl.when(slot >= 0)
        def _():
            at = jnp.maximum(slot, 0)
            pltpu.make_async_copy(points.at[0], held.at[at], reads.at[at]).wait()
            pltpu.make_async_copy(held.at[at], out, writes.at[i]).start()

        @pl.when(slot < 0)
        def _():
            pltpu.make_async_copy(zeros, out, writes.at[i]).start()

    for s in range(slots):

        @pl.when(s >= counts[0])
        def _():
            pltpu.make_async_copy(points.at[s], held.at[s], reads.at[s]).wait()

    for i, (k, out) in enumerate(targets):
        pltpu.make_async_copy(zeros, out, writes.at[i]).wait()


def stage(points, ids, counts, owners, alone, paired):
    rows, feature = points.shape[1:]
    spec = pl.BlockSpec(memory_space=pltpu.HBM)
    hbm = lambda n: pltpu.HBM((n, feature), points.dtype)
    outs = pl.pallas_call(
        functools.partial(stage_kernel, alone, paired),
        out_shape=[hbm(rows)] * len(alone) + [hbm(2 * rows)] * len(paired) + [hbm(len(paired) * rows)],
        in_specs=[spec, pl.BlockSpec(memory_space=pltpu.SMEM), spec],
        out_specs=[spec] * (len(alone) + len(paired) + 1),
        scratch_shapes=[
            pltpu.SMEM((owners,), jnp.int32),
            pltpu.SMEM(ids.shape, jnp.int32),
            pltpu.VMEM(points.shape, points.dtype),
            pltpu.VMEM((rows, feature), points.dtype),
            pltpu.SemaphoreType.DMA((points.shape[0],)),
            pltpu.SemaphoreType.DMA((len(alone) + 2 * len(paired),)),
            pltpu.SemaphoreType.DMA,
        ],
        compiler_params=pltpu.CompilerParams(vmem_limit_bytes=16 * MIB),
        name="stage",
    )(in_hbm(ids), counts, in_hbm(points))
    return dict(zip(alone, outs)), dict(zip(paired, outs[len(alone) : -1])), outs[-1]


def merge_kernel(got, *refs):
    outs, sems = refs[len(refs) // 2 : -1], refs[-1]
    rows = got.shape[0] // len(outs)
    copies = [
        pltpu.make_async_copy(got.at[pl.ds(i * rows, rows)], out.at[pl.ds(rows, rows)], sems.at[i])
        for i, out in enumerate(outs)
    ]
    for copy in copies:
        copy.start()
    for copy in copies:
        copy.wait()


def merge(keeps, got):
    spec = pl.BlockSpec(memory_space=pltpu.HBM)
    return pl.pallas_call(
        merge_kernel,
        out_shape=[pltpu.HBM(k.shape, k.dtype) for k in keeps],
        in_specs=[pl.BlockSpec(memory_space=pltpu.VMEM)] + [spec] * len(keeps),
        out_specs=[spec] * len(keeps),
        input_output_aliases={1 + i: i for i in range(len(keeps))},
        scratch_shapes=[pltpu.SemaphoreType.DMA((len(keeps),))],
        compiler_params=pltpu.CompilerParams(vmem_limit_bytes=16 * MIB),
        name="merge",
    )(in_vmem(got), *keeps)


def turns(xs):
    found, left = [], 0
    for i, x in enumerate(xs):
        start = 0
        while start < x.shape[0]:
            if not left:
                found.append([])
                left = TURN
            size = min(left, x.shape[0] - start)
            found[-1].append((i, start, start + size))
            start, left = start + size, left - size
    return found


def sums_kernel(blocks, replicas, last, *refs):
    xs, rest = refs[:blocks], refs[blocks:]
    cents, rest = rest[0], rest[1:]
    results = (1 + (replicas - 1) * HALVES) if last else replicas
    befores, outs, lts = rest[: -results - 2], rest[-results - 2 : -2], rest[-2:]
    total, feature = cents.shape
    share = total // replicas
    tile = min(TILE, share // HALVES if last else share)
    tiles = total // tile
    scale = 3.0 / math.sqrt(feature) * math.log2(math.e)
    me = lax.axis_index("copy")

    def logits(i, x, lt, high):
        here = pl.ds(i * tile, tile)
        n = x.shape[0]
        l = jnp.dot(cents[here, :], x.T, preferred_element_type=F32)
        lt[here, pl.ds(0, n)] = l
        return jnp.maximum(high, jnp.max(l.reshape(tile // 8, 8, n), axis=0))

    def exponentials(i, lt, high, norm):
        here, n = pl.ds(i * tile, tile), high.shape[1]
        e = jnp.exp2(lt[here, pl.ds(0, n)] * scale - high)
        lt[here, pl.ds(0, n)] = e
        return norm + jnp.sum(e.reshape(tile // 8, 8, n), axis=0)

    def add(i, x, lt, inverse, fresh):
        q, t = i // (share // tile), i % (share // tile)
        here = pl.ds(pl.multiple_of(lax.rem(me + q, replicas) * share + t * tile, tile), tile)
        there = pl.ds(t * tile, tile)
        weights = (lt[here, pl.ds(0, x.shape[0])] * inverse).astype(BF16)
        if last and not q:
            outs[0][there, :] = weights
            return
        s = jnp.dot(weights, x, preferred_element_type=F32)
        if not fresh:
            s = s + outs[q][there, :]
        elif befores:
            s = s + befores[q][there, :]
        if last:
            size = share // HALVES
            outs[1 + (q - 1) * HALVES + t * tile // size][pl.ds(t * tile % size, tile), :] = s
        else:
            outs[q][there, :] = s

    waiting = None
    for first, pieces in enumerate(turns(xs)):
        x = jnp.concatenate([xs[i][a:b, :] for i, a, b in pieces], axis=0)
        lt = lts[first % 2]
        n = x.shape[0]
        high = jnp.full((8, n), -jnp.inf, F32)
        if waiting:
            px, plt, phigh, fresh = waiting
            pnorm = jnp.zeros((8, px.shape[0]), F32)
        for i in range(tiles):
            high = logits(i, x, lt, high)
            if waiting:
                pnorm = exponentials(i, plt, phigh, pnorm)
        if waiting:
            inverse = 1.0 / jnp.sum(pnorm, axis=0, keepdims=True)
            for i in range(tiles):
                add(i, px, plt, inverse, fresh)
        high = jnp.max(high, axis=0, keepdims=True) * scale
        waiting = x, lt, high, first == 0
    x, lt, high, fresh = waiting
    norm = jnp.zeros((8, x.shape[0]), F32)
    for i in range(tiles):
        norm = exponentials(i, lt, high, norm)
    inverse = 1.0 / jnp.sum(norm, axis=0, keepdims=True)
    for i in range(tiles):
        add(i, x, lt, inverse, fresh)


def sums(xs, centroids, befores, replicas, last=False):
    total, feature = centroids.shape
    share = total // replicas
    points = sum(x.shape[0] for x in xs)
    assert points <= TURN or not last
    spec = pl.BlockSpec(memory_space=pltpu.VMEM)
    outs = [jax.ShapeDtypeStruct((share, feature), F32)] * replicas
    if last:
        outs = [jax.ShapeDtypeStruct((share, points), BF16)]
        outs += [jax.ShapeDtypeStruct((share // HALVES, feature), F32)] * ((replicas - 1) * HALVES)
    return pl.pallas_call(
        functools.partial(sums_kernel, len(xs), replicas, last),
        out_shape=outs,
        in_specs=[spec] * (len(xs) + 1 + len(befores)),
        out_specs=[spec] * len(outs),
        scratch_shapes=[pltpu.VMEM((total, min(TURN, points)), F32)] * 2,
        compiler_params=pltpu.CompilerParams(vmem_limit_bytes=28 * MIB),
        cost_estimate=pl.CostEstimate(flops=1024, bytes_accessed=1024, transcendentals=0),
        name="sums",
    )(*xs, centroids, *befores)


def own_kernel(blocks, *refs):
    xs, (weights, before, cents, out) = refs[:blocks], refs[blocks:]
    share = out.shape[0]
    tile = min(TILE, share)
    x = jnp.concatenate([r[...] for r in xs], axis=0)
    for t in range(share // tile):
        there = pl.ds(t * tile, tile)
        here = pl.ds(pl.multiple_of(lax.axis_index("copy") * share + t * tile, tile), tile)
        s = jnp.dot(weights[there, :], x, preferred_element_type=F32)
        out[there, :] = s + before[there, :] + cents[here, :].astype(F32)


def own(xs, weights, before, centroids):
    spec = pl.BlockSpec(memory_space=pltpu.VMEM)
    return pl.pallas_call(
        functools.partial(own_kernel, len(xs)),
        out_shape=jax.ShapeDtypeStruct(before.shape, F32),
        in_specs=[spec] * (len(xs) + 3),
        out_specs=spec,
        compiler_params=pltpu.CompilerParams(vmem_limit_bytes=28 * MIB),
        cost_estimate=pl.CostEstimate(flops=1024, bytes_accessed=1024, transcendentals=0),
        name="own",
    )(*xs, weights, before, centroids)


def close_kernel(h, terms, own, *refs):
    received, (out, held, sems) = refs[:terms], refs[-3:]
    size, feature = received[0].shape
    tile = size // 2
    copies = []
    for t in range(size // tile):
        there = pl.ds(t * tile, tile)
        v = own[pl.ds(h * size + t * tile, tile), :]
        for term in received:
            v = v + term[there, :]
        mean = jnp.mean(v * v, axis=-1, keepdims=True)
        held[there, :] = (v * lax.rsqrt(mean + 1e-06)).astype(BF16)
        copies.append(pltpu.make_async_copy(held.at[there], out.at[pl.ds(h * size + t * tile, tile)], sems.at[t]))
        copies[-1].start()
    for copy in copies:
        copy.wait()


def close(own, received, out, h):
    vmem, hbm = pl.BlockSpec(memory_space=pltpu.VMEM), pl.BlockSpec(memory_space=pl.ANY)
    terms = len(received)
    return pl.pallas_call(
        functools.partial(close_kernel, h, terms),
        out_shape=jax.ShapeDtypeStruct(own.shape, BF16),
        in_specs=[vmem] * (1 + terms) + [hbm] * len(out),
        out_specs=hbm,
        input_output_aliases={1 + terms: 0} if out else {},
        scratch_shapes=[pltpu.VMEM(received[0].shape, BF16), pltpu.SemaphoreType.DMA((2,))],
        compiler_params=pltpu.CompilerParams(vmem_limit_bytes=28 * MIB),
        cost_estimate=pl.CostEstimate(flops=1024, bytes_accessed=1024, transcendentals=0),
        name="close",
    )(own, *received, *out)


def local(points, block_ids, block_counts, centroids):
    owners = lax.axis_size("cluster")
    replicas = lax.axis_size("copy")
    assert owners >= 16 and owners & (owners - 1) == 0 and replicas % 2 == 0
    half = owners // 2
    far, paired = list(range(half, owners)), list(range(2, half, 2))
    singles, keeps, give = stage(points, block_ids, block_counts, owners, far + [0, 1], paired)
    give = lax.ppermute(give, "copy", [(k, k ^ 1) for k in range(replicas)])
    both = merge([keeps[k] for k in paired], give)
    arrived = {0: singles[0]}
    centroids = after(centroids, give)

    def send(k, *others):
        array = singles[k] if k in singles else both[paired.index(k)]
        pairs = []
        for d in range(owners):
            for r in range(replicas):
                to = d ^ (k + r % 2 if k in paired else k)
                pairs.append((d * replicas + r, to * replicas + r))
        array = after(array, *others) if others else array
        arrived[k] = lax.ppermute(array, ("cluster", "copy"), pairs)

    groups = [[0, 1, paired[0]]]
    for i in range(0, len(far) - 2, 2):
        groups.append(far[i : i + 2] + paired[1 + i // 2 : 2 + i // 2])
    groups += [far[-2:-1], far[-1:]]
    totals = []

    def work():
        group = groups[len(totals)]
        for k in group:
            if k not in arrived:
                i = paired.index(k) if k in paired else 0
                send(k, *([arrived[1 if i < 3 else paired[i - 3]]] if i else []))
        before = totals[-1] if totals else []
        last = len(totals) == len(groups) - 1
        totals.append(sums([arrived[k] for k in group], centroids, before, replicas, last))

    for i, k in enumerate(far):
        others = [arrived[far[i - 3]]] if i >= 3 else []
        if i >= 6:
            ahead = min(i - 6, i // 2 - 2)
            while len(totals) <= ahead:
                work()
            others.append(totals[ahead][0])
        send(k, *others)
    while len(totals) < len(groups):
        work()
    before, (weights, *shares) = totals[-2:]

    mine = own([arrived[k] for k in groups[-1]], weights, before[0], centroids)
    received = []
    for h in range(HALVES):
        received.append([
            lax.ppermute(shares[(r - 1) * HALVES + h], "copy", [(i, (i + r) % replicas) for i in range(replicas)])
            for r in range(1, replicas)
        ])
    out = []
    for h in range(HALVES):
        out = [close(mine, received[h], out, h)]
    return out[0]


def solution(mesh):
    return jax.shard_map(
        local,
        mesh=mesh,
        in_specs=(
            P(("cluster", "copy"), None, None),
            P(("cluster", "copy")),
            P(("cluster", "copy")),
            P("cluster", None),
        ),
        out_specs=P(("cluster", "copy"), None),
        check_vma=False,
    )
```

```python
import functools
import math

import jax
import jax.numpy as jnp
from jax import lax
from jax.experimental import pallas as pl
from jax.experimental.pallas import tpu as pltpu
from jax.sharding import PartitionSpec as P

F32 = jnp.float32
BF16 = jnp.bfloat16
TILE = 512
TURN = 256
MIB = 1 << 20
HALVES = 2


def in_hbm(array):
    return pltpu.with_memory_space_constraint(array, pltpu.HBM)


def in_vmem(array):
    return pltpu.with_memory_space_constraint(array, pltpu.VMEM)


def after(array, *others):
    return lax.optimization_barrier((array, *others))[0]


def stage_kernel(alone, paired, ids_in, counts, points, *refs):
    singles, rest = refs[: len(alone)], refs[len(alone) :]
    kept, give, where, ids, held, zeros, reads, writes, small = rest
    slots, rows = points.shape[:2]
    me, core = lax.axis_index("cluster"), lax.rem(lax.axis_index("copy"), 2)
    ids_copy = pltpu.make_async_copy(ids_in, ids, small)
    ids_copy.start()
    for s in range(slots):
        pltpu.make_async_copy(points.at[s], held.at[s], reads.at[s]).start()
    for o in range(where.shape[0]):
        where[o] = -1
    zeros[...] = jnp.zeros_like(zeros)
    ids_copy.wait()
    for s in range(slots):

        @pl.when(s < counts[0])
        def _():
            where[ids[s]] = s

    targets = [(k, out) for k, out in zip(alone, singles)]
    targets += [(k + 1 - core, give.at[pl.ds(i * rows, rows)]) for i, k in enumerate(paired)]
    targets += [(k + core, kept.at[pl.ds(i * rows, rows)]) for i, k in enumerate(paired)]
    targets += [(0, kept.at[pl.ds(len(paired) * rows, rows)])]
    for i, (k, out) in enumerate(targets):
        slot = where[me ^ k]

        @pl.when(slot >= 0)
        def _():
            at = jnp.maximum(slot, 0)
            pltpu.make_async_copy(points.at[0], held.at[at], reads.at[at]).wait()
            pltpu.make_async_copy(held.at[at], out, writes.at[i]).start()

        @pl.when(slot < 0)
        def _():
            pltpu.make_async_copy(zeros, out, writes.at[i]).start()

    for s in range(slots):

        @pl.when(s >= counts[0])
        def _():
            pltpu.make_async_copy(points.at[s], held.at[s], reads.at[s]).wait()

    for i, (k, out) in enumerate(targets):
        pltpu.make_async_copy(zeros, out, writes.at[i]).wait()


def stage(points, ids, counts, owners, alone, paired):
    rows, feature = points.shape[1:]
    spec = pl.BlockSpec(memory_space=pltpu.HBM)
    hbm = lambda n: pltpu.HBM((n, feature), points.dtype)
    outs = pl.pallas_call(
        functools.partial(stage_kernel, alone, paired),
        out_shape=[hbm(rows)] * len(alone) + [hbm((1 + len(paired)) * rows), hbm(len(paired) * rows)],
        in_specs=[spec, pl.BlockSpec(memory_space=pltpu.SMEM), spec],
        out_specs=[spec] * (len(alone) + 2),
        scratch_shapes=[
            pltpu.SMEM((owners,), jnp.int32),
            pltpu.SMEM(ids.shape, jnp.int32),
            pltpu.VMEM(points.shape, points.dtype),
            pltpu.VMEM((rows, feature), points.dtype),
            pltpu.SemaphoreType.DMA((points.shape[0],)),
            pltpu.SemaphoreType.DMA((len(alone) + 2 * len(paired) + 1,)),
            pltpu.SemaphoreType.DMA,
        ],
        compiler_params=pltpu.CompilerParams(vmem_limit_bytes=16 * MIB),
        name="stage",
    )(in_hbm(ids), counts, in_hbm(points))
    return dict(zip(alone, outs)), outs[-2], outs[-1]


def merge_kernel(kept, got, *refs):
    outs, own, sems = refs[:-2], refs[-2], refs[-1]
    rows = own.shape[0]
    copies = []
    for i, out in enumerate(outs):
        for j, source in enumerate((kept, got)):
            there = out.at[pl.ds(j * rows, rows)]
            copies.append(pltpu.make_async_copy(source.at[pl.ds(i * rows, rows)], there, sems.at[i, j]))
    copies.append(pltpu.make_async_copy(kept.at[pl.ds(len(outs) * rows, rows)], own, sems.at[len(outs), 0]))
    for copy in copies:
        copy.start()
    for copy in copies:
        copy.wait()


def merge(kept, got, rows):
    pairs = got.shape[0] // rows
    hbm, vmem = pl.BlockSpec(memory_space=pltpu.HBM), pl.BlockSpec(memory_space=pltpu.VMEM)
    return pl.pallas_call(
        merge_kernel,
        out_shape=[pltpu.HBM((2 * rows, got.shape[1]), got.dtype)] * pairs
        + [jax.ShapeDtypeStruct((rows, got.shape[1]), got.dtype)],
        in_specs=[vmem, vmem],
        out_specs=[hbm] * pairs + [vmem],
        scratch_shapes=[pltpu.SemaphoreType.DMA((pairs + 1, 2))],
        compiler_params=pltpu.CompilerParams(vmem_limit_bytes=16 * MIB),
        name="merge",
    )(in_vmem(kept), in_vmem(got))


def turns(xs):
    found, left = [], 0
    for i, x in enumerate(xs):
        start = 0
        while start < x.shape[0]:
            if not left:
                found.append([])
                left = TURN
            size = min(left, x.shape[0] - start)
            found[-1].append((i, start, start + size))
            start, left = start + size, left - size
    return found


def sums_kernel(blocks, replicas, last, *refs):
    xs, rest = refs[:blocks], refs[blocks:]
    cents, rest = rest[0], rest[1:]
    results = (1 + (replicas - 1) * HALVES) if last else replicas
    befores, outs, lts = rest[: -results - 2], rest[-results - 2 : -2], rest[-2:]
    total, feature = cents.shape
    share = total // replicas
    tile = min(TILE, share // HALVES if last else share)
    tiles = total // tile
    scale = 3.0 / math.sqrt(feature) * math.log2(math.e)
    me = lax.axis_index("copy")

    def logits(i, x, lt, high):
        here = pl.ds(i * tile, tile)
        n = x.shape[0]
        l = jnp.dot(cents[here, :], x.T, preferred_element_type=F32)
        lt[here, pl.ds(0, n)] = l
        return jnp.maximum(high, jnp.max(l.reshape(tile // 8, 8, n), axis=0))

    def exponentials(i, lt, high, norm):
        here, n = pl.ds(i * tile, tile), high.shape[1]
        e = jnp.exp2(lt[here, pl.ds(0, n)] * scale - high)
        lt[here, pl.ds(0, n)] = e
        return norm + jnp.sum(e.reshape(tile // 8, 8, n), axis=0)

    def add(i, x, lt, inverse, fresh):
        q, t = i // (share // tile), i % (share // tile)
        here = pl.ds(pl.multiple_of(lax.rem(me + q, replicas) * share + t * tile, tile), tile)
        there = pl.ds(t * tile, tile)
        weights = (lt[here, pl.ds(0, x.shape[0])] * inverse).astype(BF16)
        if last and not q:
            outs[0][there, :] = weights
            return
        s = jnp.dot(weights, x, preferred_element_type=F32)
        if not fresh:
            s = s + outs[q][there, :]
        elif befores:
            s = s + befores[q][there, :]
        if last:
            size = share // HALVES
            outs[1 + (q - 1) * HALVES + t * tile // size][pl.ds(t * tile % size, tile), :] = s
        else:
            outs[q][there, :] = s

    waiting = None
    for first, pieces in enumerate(turns(xs)):
        x = jnp.concatenate([xs[i][a:b, :] for i, a, b in pieces], axis=0)
        lt = lts[first % 2]
        n = x.shape[0]
        high = jnp.full((8, n), -jnp.inf, F32)
        if waiting:
            px, plt, phigh, fresh = waiting
            pnorm = jnp.zeros((8, px.shape[0]), F32)
        for i in range(tiles):
            high = logits(i, x, lt, high)
            if waiting:
                pnorm = exponentials(i, plt, phigh, pnorm)
        if waiting:
            inverse = 1.0 / jnp.sum(pnorm, axis=0, keepdims=True)
            for i in range(tiles):
                add(i, px, plt, inverse, fresh)
        high = jnp.max(high, axis=0, keepdims=True) * scale
        waiting = x, lt, high, first == 0
    x, lt, high, fresh = waiting
    norm = jnp.zeros((8, x.shape[0]), F32)
    for i in range(tiles):
        norm = exponentials(i, lt, high, norm)
    inverse = 1.0 / jnp.sum(norm, axis=0, keepdims=True)
    for i in range(tiles):
        add(i, x, lt, inverse, fresh)


def sums(xs, centroids, befores, replicas, last=False):
    total, feature = centroids.shape
    share = total // replicas
    points = sum(x.shape[0] for x in xs)
    assert points <= TURN or not last
    spec = pl.BlockSpec(memory_space=pltpu.VMEM)
    outs = [jax.ShapeDtypeStruct((share, feature), F32)] * replicas
    if last:
        outs = [jax.ShapeDtypeStruct((share, points), BF16)]
        outs += [jax.ShapeDtypeStruct((share // HALVES, feature), F32)] * ((replicas - 1) * HALVES)
    return pl.pallas_call(
        functools.partial(sums_kernel, len(xs), replicas, last),
        out_shape=outs,
        in_specs=[spec] * (len(xs) + 1 + len(befores)),
        out_specs=[spec] * len(outs),
        scratch_shapes=[pltpu.VMEM((total, min(TURN, points)), F32)] * 2,
        compiler_params=pltpu.CompilerParams(vmem_limit_bytes=28 * MIB),
        cost_estimate=pl.CostEstimate(flops=1024, bytes_accessed=1024, transcendentals=0),
        name="sums",
    )(*xs, centroids, *befores)


def own_kernel(blocks, *refs):
    xs, (weights, before, cents, out) = refs[:blocks], refs[blocks:]
    share = out.shape[0]
    tile = min(TILE, share)
    x = jnp.concatenate([r[...] for r in xs], axis=0)
    for t in range(share // tile):
        there = pl.ds(t * tile, tile)
        here = pl.ds(pl.multiple_of(lax.axis_index("copy") * share + t * tile, tile), tile)
        s = jnp.dot(weights[there, :], x, preferred_element_type=F32)
        out[there, :] = s + before[there, :] + cents[here, :].astype(F32)


def own(xs, weights, before, centroids):
    spec = pl.BlockSpec(memory_space=pltpu.VMEM)
    return pl.pallas_call(
        functools.partial(own_kernel, len(xs)),
        out_shape=jax.ShapeDtypeStruct(before.shape, F32),
        in_specs=[spec] * (len(xs) + 3),
        out_specs=spec,
        compiler_params=pltpu.CompilerParams(vmem_limit_bytes=28 * MIB),
        cost_estimate=pl.CostEstimate(flops=1024, bytes_accessed=1024, transcendentals=0),
        name="own",
    )(*xs, weights, before, centroids)


def close_kernel(h, terms, own, *refs):
    received, (out, held, sems) = refs[:terms], refs[-3:]
    size, feature = received[0].shape
    tile = size // 2
    copies = []
    for t in range(size // tile):
        there = pl.ds(t * tile, tile)
        v = own[pl.ds(h * size + t * tile, tile), :]
        for term in received:
            v = v + term[there, :]
        mean = jnp.mean(v * v, axis=-1, keepdims=True)
        held[there, :] = (v * lax.rsqrt(mean + 1e-06)).astype(BF16)
        copies.append(pltpu.make_async_copy(held.at[there], out.at[pl.ds(h * size + t * tile, tile)], sems.at[t]))
        copies[-1].start()
    for copy in copies:
        copy.wait()


def close(own, received, out, h):
    vmem, hbm = pl.BlockSpec(memory_space=pltpu.VMEM), pl.BlockSpec(memory_space=pl.ANY)
    terms = len(received)
    return pl.pallas_call(
        functools.partial(close_kernel, h, terms),
        out_shape=jax.ShapeDtypeStruct(own.shape, BF16),
        in_specs=[vmem] * (1 + terms) + [hbm] * len(out),
        out_specs=hbm,
        input_output_aliases={1 + terms: 0} if out else {},
        scratch_shapes=[pltpu.VMEM(received[0].shape, BF16), pltpu.SemaphoreType.DMA((2,))],
        compiler_params=pltpu.CompilerParams(vmem_limit_bytes=28 * MIB),
        cost_estimate=pl.CostEstimate(flops=1024, bytes_accessed=1024, transcendentals=0),
        name="close",
    )(own, *received, *out)


def local(points, block_ids, block_counts, centroids):
    owners = lax.axis_size("cluster")
    replicas = lax.axis_size("copy")
    assert owners >= 16 and owners & (owners - 1) == 0 and replicas % 2 == 0
    half = owners // 2
    far, paired = list(range(half, owners)), list(range(2, half, 2))
    singles, kept, give = stage(points, block_ids, block_counts, owners, far + [1], paired)
    give = lax.ppermute(give, "copy", [(k, k ^ 1) for k in range(replicas)])
    *both, mine = merge(kept, give, points.shape[1])
    arrived = {0: mine}
    centroids = after(centroids, give)

    def send(k, *others):
        array = singles[k] if k in singles else both[paired.index(k)]
        pairs = []
        for d in range(owners):
            for r in range(replicas):
                to = d ^ (k + r % 2 if k in paired else k)
                pairs.append((d * replicas + r, to * replicas + r))
        array = after(array, *others) if others else array
        arrived[k] = lax.ppermute(array, ("cluster", "copy"), pairs)

    groups = [[0, 1, paired[0]]]
    for i in range(0, len(far) - 2, 2):
        groups.append(far[i : i + 2] + paired[1 + i // 2 : 2 + i // 2])
    groups += [far[-2:-1], far[-1:]]
    totals = []

    def work():
        group = groups[len(totals)]
        for k in group:
            if k not in arrived:
                i = paired.index(k) if k in paired else 0
                send(k, *([arrived[1 if i < 3 else paired[i - 3]]] if i else []))
        before = totals[-1] if totals else []
        last = len(totals) == len(groups) - 1
        totals.append(sums([arrived[k] for k in group], centroids, before, replicas, last))

    for i, k in enumerate(far):
        others = [arrived[far[i - 3]]] if i >= 3 else []
        if i >= 6:
            ahead = min(i - 6, i // 2 - 2)
            while len(totals) <= ahead:
                work()
            others.append(totals[ahead][0])
        send(k, *others)
    while len(totals) < len(groups):
        work()
    before, (weights, *shares) = totals[-2:]

    mine = own([arrived[k] for k in groups[-1]], weights, before[0], centroids)
    received = []
    for h in range(HALVES):
        received.append([
            lax.ppermute(shares[(r - 1) * HALVES + h], "copy", [(i, (i + r) % replicas) for i in range(replicas)])
            for r in range(1, replicas)
        ])
    out = []
    for h in range(HALVES):
        out = [close(mine, received[h], out, h)]
    return out[0]


def solution(mesh):
    return jax.shard_map(
        local,
        mesh=mesh,
        in_specs=(
            P(("cluster", "copy"), None, None),
            P(("cluster", "copy")),
            P(("cluster", "copy")),
            P("cluster", None),
        ),
        out_specs=P(("cluster", "copy"), None),
        check_vma=False,
    )
```

```python
import functools
import math

import jax
import jax.numpy as jnp
from jax import lax
from jax.experimental import pallas as pl
from jax.experimental.pallas import tpu as pltpu
from jax.sharding import PartitionSpec as P

F32 = jnp.float32
BF16 = jnp.bfloat16
TILE = 512
TURN = 256
MIB = 1 << 20
HALVES = 2


def in_hbm(array):
    return pltpu.with_memory_space_constraint(array, pltpu.HBM)


def in_vmem(array):
    return pltpu.with_memory_space_constraint(array, pltpu.VMEM)


def after(array, *others):
    return lax.optimization_barrier((array, *others))[0]


def stage_kernel(alone, paired, ids_in, counts, points, *refs):
    singles, rest = refs[: len(alone)], refs[len(alone) :]
    kept, give, where, ids, held, zeros, reads, writes, small = rest
    slots, rows = points.shape[:2]
    me, core = lax.axis_index("cluster"), lax.rem(lax.axis_index("copy"), 2)
    ids_copy = pltpu.make_async_copy(ids_in, ids, small)
    ids_copy.start()
    for s in range(slots):
        pltpu.make_async_copy(points.at[s], held.at[s], reads.at[s]).start()
    for o in range(where.shape[0]):
        where[o] = -1
    zeros[...] = jnp.zeros_like(zeros)
    ids_copy.wait()
    for s in range(slots):

        @pl.when(s < counts[0])
        def _():
            where[ids[s]] = s

    targets = [(k, out) for k, out in zip(alone, singles)]
    targets += [(k + 1 - core, give.at[pl.ds(i * rows, rows)]) for i, k in enumerate(paired)]
    targets += [(k + core, kept.at[pl.ds(i * rows, rows)]) for i, k in enumerate(paired)]
    targets += [(0, kept.at[pl.ds(len(paired) * rows, rows)])]
    for i, (k, out) in enumerate(targets):
        slot = where[me ^ k]

        @pl.when(slot >= 0)
        def _():
            at = jnp.maximum(slot, 0)
            pltpu.make_async_copy(points.at[0], held.at[at], reads.at[at]).wait()
            pltpu.make_async_copy(held.at[at], out, writes.at[i]).start()

        @pl.when(slot < 0)
        def _():
            pltpu.make_async_copy(zeros, out, writes.at[i]).start()

    for s in range(slots):

        @pl.when(s >= counts[0])
        def _():
            pltpu.make_async_copy(points.at[s], held.at[s], reads.at[s]).wait()

    for i, (k, out) in enumerate(targets):
        pltpu.make_async_copy(zeros, out, writes.at[i]).wait()


def stage(points, ids, counts, owners, alone, paired):
    rows, feature = points.shape[1:]
    spec = pl.BlockSpec(memory_space=pltpu.HBM)
    hbm = lambda n: pltpu.HBM((n, feature), points.dtype)
    outs = pl.pallas_call(
        functools.partial(stage_kernel, alone, paired),
        out_shape=[hbm(rows)] * len(alone) + [hbm((1 + len(paired)) * rows), hbm(len(paired) * rows)],
        in_specs=[spec, pl.BlockSpec(memory_space=pltpu.SMEM), spec],
        out_specs=[spec] * (len(alone) + 2),
        scratch_shapes=[
            pltpu.SMEM((owners,), jnp.int32),
            pltpu.SMEM(ids.shape, jnp.int32),
            pltpu.VMEM(points.shape, points.dtype),
            pltpu.VMEM((rows, feature), points.dtype),
            pltpu.SemaphoreType.DMA((points.shape[0],)),
            pltpu.SemaphoreType.DMA((len(alone) + 2 * len(paired) + 1,)),
            pltpu.SemaphoreType.DMA,
        ],
        compiler_params=pltpu.CompilerParams(vmem_limit_bytes=16 * MIB),
        name="stage",
    )(in_hbm(ids), counts, in_hbm(points))
    return dict(zip(alone, outs)), outs[-2], outs[-1]


def merge_kernel(kept, got, *refs):
    outs, own, sems = refs[:-2], refs[-2], refs[-1]
    rows = own.shape[0]
    copies = []
    for i, out in enumerate(outs):
        for j, source in enumerate((kept, got)):
            there = out.at[pl.ds(j * rows, rows)]
            copies.append(pltpu.make_async_copy(source.at[pl.ds(i * rows, rows)], there, sems.at[i, j]))
    copies.append(pltpu.make_async_copy(kept.at[pl.ds(len(outs) * rows, rows)], own, sems.at[len(outs), 0]))
    for copy in copies:
        copy.start()
    for copy in copies:
        copy.wait()


def merge(kept, got, rows):
    pairs = got.shape[0] // rows
    hbm, vmem = pl.BlockSpec(memory_space=pltpu.HBM), pl.BlockSpec(memory_space=pltpu.VMEM)
    return pl.pallas_call(
        merge_kernel,
        out_shape=[pltpu.HBM((2 * rows, got.shape[1]), got.dtype)] * pairs
        + [jax.ShapeDtypeStruct((rows, got.shape[1]), got.dtype)],
        in_specs=[vmem, vmem],
        out_specs=[hbm] * pairs + [vmem],
        scratch_shapes=[pltpu.SemaphoreType.DMA((pairs + 1, 2))],
        compiler_params=pltpu.CompilerParams(vmem_limit_bytes=16 * MIB),
        name="merge",
    )(in_vmem(kept), in_vmem(got))


def turns(xs):
    found, left = [], 0
    for i, x in enumerate(xs):
        start = 0
        while start < x.shape[0]:
            if not left:
                found.append([])
                left = TURN
            size = min(left, x.shape[0] - start)
            found[-1].append((i, start, start + size))
            start, left = start + size, left - size
    return found


def sums_kernel(blocks, replicas, last, *refs):
    xs, rest = refs[:blocks], refs[blocks:]
    cents, rest = rest[0], rest[1:]
    results = (1 + (replicas - 1) * HALVES) if last else replicas
    befores, outs, lts = rest[: -results - 2], rest[-results - 2 : -2], rest[-2:]
    total, feature = cents.shape
    share = total // replicas
    tile = min(TILE, share // HALVES if last else share)
    tiles = total // tile
    scale = 3.0 / math.sqrt(feature) * math.log2(math.e)
    me = lax.axis_index("copy")

    def logits(i, x, lt, high):
        here = pl.ds(i * tile, tile)
        n = x.shape[0]
        l = jnp.dot(cents[here, :], x.T, preferred_element_type=F32)
        lt[here, pl.ds(0, n)] = l
        return jnp.maximum(high, jnp.max(l.reshape(tile // 8, 8, n), axis=0))

    def exponentials(i, lt, high, norm):
        here, n = pl.ds(i * tile, tile), high.shape[1]
        e = jnp.exp2(lt[here, pl.ds(0, n)] * scale - high)
        lt[here, pl.ds(0, n)] = e
        return norm + jnp.sum(e.reshape(tile // 8, 8, n), axis=0)

    def add(i, x, lt, inverse, fresh):
        q, t = i // (share // tile), i % (share // tile)
        here = pl.ds(pl.multiple_of(lax.rem(me + q, replicas) * share + t * tile, tile), tile)
        there = pl.ds(t * tile, tile)
        weights = (lt[here, pl.ds(0, x.shape[0])] * inverse).astype(BF16)
        if last and not q:
            outs[0][there, :] = weights
            return
        s = jnp.dot(weights, x, preferred_element_type=F32)
        if not fresh:
            s = s + outs[q][there, :]
        elif befores:
            s = s + befores[q][there, :]
        if last:
            size = share // HALVES
            outs[1 + (q - 1) * HALVES + t * tile // size][pl.ds(t * tile % size, tile), :] = s
        else:
            outs[q][there, :] = s

    waiting = None
    for first, pieces in enumerate(turns(xs)):
        x = jnp.concatenate([xs[i][a:b, :] for i, a, b in pieces], axis=0)
        lt = lts[first % 2]
        n = x.shape[0]
        high = jnp.full((8, n), -jnp.inf, F32)
        if waiting:
            px, plt, phigh, fresh = waiting
            pnorm = jnp.zeros((8, px.shape[0]), F32)
        for i in range(tiles):
            high = logits(i, x, lt, high)
            if waiting:
                pnorm = exponentials(i, plt, phigh, pnorm)
        if waiting:
            inverse = 1.0 / jnp.sum(pnorm, axis=0, keepdims=True)
            for i in range(tiles):
                add(i, px, plt, inverse, fresh)
        high = jnp.max(high, axis=0, keepdims=True) * scale
        waiting = x, lt, high, first == 0
    x, lt, high, fresh = waiting
    norm = jnp.zeros((8, x.shape[0]), F32)
    for i in range(tiles):
        norm = exponentials(i, lt, high, norm)
    inverse = 1.0 / jnp.sum(norm, axis=0, keepdims=True)
    for i in range(tiles):
        add(i, x, lt, inverse, fresh)


def sums(xs, centroids, befores, replicas, last=False):
    total, feature = centroids.shape
    share = total // replicas
    points = sum(x.shape[0] for x in xs)
    assert points <= TURN or not last
    spec = pl.BlockSpec(memory_space=pltpu.VMEM)
    outs = [jax.ShapeDtypeStruct((share, feature), F32)] * replicas
    if last:
        outs = [jax.ShapeDtypeStruct((share, points), BF16)]
        outs += [jax.ShapeDtypeStruct((share // HALVES, feature), F32)] * ((replicas - 1) * HALVES)
    return pl.pallas_call(
        functools.partial(sums_kernel, len(xs), replicas, last),
        out_shape=outs,
        in_specs=[spec] * (len(xs) + 1 + len(befores)),
        out_specs=[spec] * len(outs),
        scratch_shapes=[pltpu.VMEM((total, min(TURN, points)), F32)] * 2,
        compiler_params=pltpu.CompilerParams(vmem_limit_bytes=28 * MIB),
        cost_estimate=pl.CostEstimate(flops=1024, bytes_accessed=1024, transcendentals=0),
        name="sums",
    )(*xs, centroids, *befores)


def own_kernel(blocks, *refs):
    xs, (weights, before, cents, out) = refs[:blocks], refs[blocks:]
    share = out.shape[0]
    tile = min(TILE, share)
    x = jnp.concatenate([r[...] for r in xs], axis=0)
    for t in range(share // tile):
        there = pl.ds(t * tile, tile)
        here = pl.ds(pl.multiple_of(lax.axis_index("copy") * share + t * tile, tile), tile)
        s = jnp.dot(weights[there, :], x, preferred_element_type=F32)
        out[there, :] = s + before[there, :] + cents[here, :].astype(F32)


def own(xs, weights, before, centroids):
    spec = pl.BlockSpec(memory_space=pltpu.VMEM)
    return pl.pallas_call(
        functools.partial(own_kernel, len(xs)),
        out_shape=jax.ShapeDtypeStruct(before.shape, F32),
        in_specs=[spec] * (len(xs) + 3),
        out_specs=spec,
        compiler_params=pltpu.CompilerParams(vmem_limit_bytes=28 * MIB),
        cost_estimate=pl.CostEstimate(flops=1024, bytes_accessed=1024, transcendentals=0),
        name="own",
    )(*xs, weights, before, centroids)


def close_kernel(h, terms, own, *refs):
    received, (out, held, sems) = refs[:terms], refs[-3:]
    size, feature = received[0].shape
    tile = size // 2
    copies = []
    for t in range(size // tile):
        there = pl.ds(t * tile, tile)
        v = own[pl.ds(h * size + t * tile, tile), :]
        for term in received:
            v = v + term[there, :]
        mean = jnp.mean(v * v, axis=-1, keepdims=True)
        held[there, :] = (v * lax.rsqrt(mean + 1e-06)).astype(BF16)
        copies.append(pltpu.make_async_copy(held.at[there], out.at[pl.ds(h * size + t * tile, tile)], sems.at[t]))
        copies[-1].start()
    for copy in copies:
        copy.wait()


def close(own, received, out, h):
    vmem, hbm = pl.BlockSpec(memory_space=pltpu.VMEM), pl.BlockSpec(memory_space=pl.ANY)
    terms = len(received)
    return pl.pallas_call(
        functools.partial(close_kernel, h, terms),
        out_shape=jax.ShapeDtypeStruct(own.shape, BF16),
        in_specs=[vmem] * (1 + terms) + [hbm] * len(out),
        out_specs=hbm,
        input_output_aliases={1 + terms: 0} if out else {},
        scratch_shapes=[pltpu.VMEM(received[0].shape, BF16), pltpu.SemaphoreType.DMA((2,))],
        compiler_params=pltpu.CompilerParams(vmem_limit_bytes=28 * MIB),
        cost_estimate=pl.CostEstimate(flops=1024, bytes_accessed=1024, transcendentals=0),
        name="close",
    )(own, *received, *out)


def local(points, block_ids, block_counts, centroids):
    owners = lax.axis_size("cluster")
    replicas = lax.axis_size("copy")
    assert owners >= 16 and owners & (owners - 1) == 0 and replicas % 2 == 0
    half = owners // 2
    far = [half + (i & ~3 | (i & 1) << 1 | i >> 1 & 1) for i in range(half)]
    paired = list(range(2, half, 2))
    singles, kept, give = stage(points, block_ids, block_counts, owners, far + [1], paired)
    give = lax.ppermute(give, "copy", [(k, k ^ 1) for k in range(replicas)])
    *both, mine = merge(kept, give, points.shape[1])
    arrived = {0: mine}
    centroids = after(centroids, give)

    def send(k, *others):
        array = singles[k] if k in singles else both[paired.index(k)]
        pairs = []
        for d in range(owners):
            for r in range(replicas):
                to = d ^ (k + r % 2 if k in paired else k)
                pairs.append((d * replicas + r, to * replicas + r))
        array = after(array, *others) if others else array
        arrived[k] = lax.ppermute(array, ("cluster", "copy"), pairs)

    groups = [[0, 1, paired[0]]]
    for i in range(0, len(far) - 2, 2):
        groups.append(far[i : i + 2] + paired[1 + i // 2 : 2 + i // 2])
    groups += [far[-2:-1], far[-1:]]
    totals = []

    def work():
        group = groups[len(totals)]
        for k in group:
            if k not in arrived:
                i = paired.index(k) if k in paired else 0
                send(k, *([arrived[1 if i < 3 else paired[i - 3]]] if i else []))
        before = totals[-1] if totals else []
        last = len(totals) == len(groups) - 1
        totals.append(sums([arrived[k] for k in group], centroids, before, replicas, last))

    for i, k in enumerate(far):
        others = [arrived[far[i - 3]]] if i >= 3 else []
        if i >= 6:
            ahead = min(i - 6, i // 2 - 2)
            while len(totals) <= ahead:
                work()
            others.append(totals[ahead][0])
        send(k, *others)
    while len(totals) < len(groups):
        work()
    before, (weights, *shares) = totals[-2:]

    mine = own([arrived[k] for k in groups[-1]], weights, before[0], centroids)
    received = []
    for h in range(HALVES):
        received.append([
            lax.ppermute(shares[(r - 1) * HALVES + h], "copy", [(i, (i + r) % replicas) for i in range(replicas)])
            for r in range(1, replicas)
        ])
    out = []
    for h in range(HALVES):
        out = [close(mine, received[h], out, h)]
    return out[0]


def solution(mesh):
    return jax.shard_map(
        local,
        mesh=mesh,
        in_specs=(
            P(("cluster", "copy"), None, None),
            P(("cluster", "copy")),
            P(("cluster", "copy")),
            P("cluster", None),
        ),
        out_specs=P(("cluster", "copy"), None),
        check_vma=False,
    )
```
